32 devices in a mesh: row: 8 (over z, x), col: 4 (over y, core).
Axes of the slice: x: 2, y: 2, z: 4, core: 2. Of those that a mesh axis runs over, the one named last changes fastest.
Arguments:
- factor: float32 [2, 2048, 2, 1024], P(None, 'row', None, 'col'), may hold values from -5 to 5, as said below
- update: float32 [2, 2048, 512], P(None, 'row', 'col'), may hold values from -1.5 to 1.5
Outputs:
- updated_factor: float32 [2, 2048, 2, 1024], P(None, 'row', None, 'col')
The draws below stay inside these ranges and needn't reach their ends.
Inputs may be any that keep to these rules, and one draw needn't show every extreme that they name: `factor`: in the first 2048 rows, entries to the right of the diagonal are zero and diagonal entries are positive.
All inputs are finite; a program needn't handle non-finite values.
Results may differ from the reference program's by a relative error of at most 0.0003.
Values sent between devices are 32-bit elements; how exact they have to be, the bound alone decides.
A program may use at most 128 MiB of HBM per device.

```python
import jax
import jax.numpy as jnp
from jax import lax

PANEL = 1024
PANELS = 2
K = 512
RT = 2
SPAN = 2048


def draw_factor(key, part):
    key_base, key_diag = jax.random.split(key, 2)
    shape = (RT, SPAN, PANELS, PANEL)
    global_row = jnp.arange(RT, dtype=jnp.int32)[:, None, None, None] * SPAN + jnp.arange(SPAN, dtype=jnp.int32)[None, :, None, None]
    global_col = jnp.arange(PANELS, dtype=jnp.int32)[None, None, :, None] * PANEL + jnp.arange(PANEL, dtype=jnp.int32)[None, None, None, :]
    diag_span = PANELS * PANEL
    base = jnp.clip(jax.random.normal(key_base, shape, jnp.float32), -5.0, 5.0)
    diagonal = jax.random.uniform(key_diag, shape, jnp.float32, 2.0, 4.0)
    lower_part = base * jnp.float32(diag_span) ** (-0.5)
    inside_value = jnp.where(global_col < global_row, lower_part, jnp.where(global_col == global_row, diagonal, jnp.zeros_like(base)))
    return jnp.where(global_row < diag_span, inside_value, base)


def levels(stream_key, dims, pieces, smallest, high):
    level, own = 1.0, jax.random.fold_in(stream_key, 6)
    for axis_at, blocks in pieces:
        steps = jnp.exp(jax.random.uniform(jax.random.fold_in(own, axis_at), (blocks,), jnp.float32, smallest / len(pieces), high / len(pieces)))
        level = level * jnp.repeat(steps, dims[axis_at] // blocks).reshape([-1 if axis == axis_at else 1 for axis in range(len(dims))])
    return level


def scatter_about(key, extent, width, limit, pieces=(), kind=jnp.bfloat16):
    values = width * jax.random.normal(key, extent, jnp.float32)
    if pieces:
        values = values * levels(key, extent, pieces, -0.22, 0.18)
    return jnp.clip(values, -limit, limit).astype(kind)


def setup_inputs(seed: int = 0) -> dict:
    seeds = jax.random.split(jax.random.key(seed), 3)
    return {
        "factor": draw_factor(jax.random.fold_in(seeds[2], 71), 0),
        "update": scatter_about(seeds[1], (RT, SPAN, K), 0.25, 1.5, ((1, 8), (2, 4)), jnp.float32),
    }


def reference(factor, update):
    blocks, cycle_rows, panels, panel_cols = factor.shape
    total_rows = blocks * cycle_rows
    factor_width = panels * panel_cols
    joined = jnp.concatenate([factor.reshape(total_rows, factor_width), update.reshape(total_rows, update.shape[2])], axis=1)
    outputs = []
    for panel_idx in range(panels):
        row_start = panel_idx * panel_cols
        row_end = row_start + panel_cols
        chosen = jnp.concatenate([joined[:, :row_end], joined[:, factor_width:]], axis=1)
        panel_rows = chosen[row_start:row_end]
        earlier = [prev_out[row_start:row_end] for prev_out in outputs]
        lhs_block = jnp.concatenate([panel_rows] + earlier, axis=1)
        rhs_block = jnp.concatenate([panel_rows] + [-entry for entry in earlier], axis=1)
        gram_block = jnp.dot(lhs_block.astype(jnp.float32), rhs_block.T.astype(jnp.float32), precision=lax.Precision.HIGHEST, preferred_element_type=jnp.float32)
        factor_block = jnp.linalg.cholesky(gram_block)
        solved = lax.linalg.triangular_solve(factor_block, rhs_block, left_side=True, lower=True)
        left_rows = jnp.concatenate([chosen] + outputs, axis=1)
        outputs.append(jnp.dot(left_rows.astype(jnp.float32), solved.T.astype(jnp.float32), precision=lax.Precision.HIGHEST, preferred_element_type=jnp.float32))
    stacked = jnp.stack(outputs, axis=1)
    global_row = jnp.arange(total_rows, dtype=jnp.int32)
    global_col = jnp.arange(panels, dtype=jnp.int32)[:, None] * panel_cols + jnp.arange(panel_cols, dtype=jnp.int32)[None, :]
    inside = global_col[None, :, :] <= global_row[:, None, None]
    result = jnp.where(inside, stacked, jnp.zeros_like(stacked))
    return result.reshape(blocks, cycle_rows, panels, panel_cols)
```

```python
import functools

import jax
import jax.numpy as jnp
from jax import lax
from jax.experimental import pallas as pl
from jax.experimental.pallas import tpu as pltpu
from jax.sharding import PartitionSpec as P

PANEL = 1024
PANELS = 2
B=256; H=128; GRP=8
NN=(((1,),(0,)),((),()))
NT=(((1,),(1,)),((),())); TN=(((0,),(0,)),((),()))
def split(x):
    hi=x.astype(jnp.bfloat16); return hi,(x-hi.astype(jnp.float32)).astype(jnp.bfloat16)
def dot3(a,b,dims=NT):
    (ah,al),(bh,bl)=a,b
    d=functools.partial(lax.dot_general,dimension_numbers=dims,preferred_element_type=jnp.float32)
    return d(ah,bh)+(d(ah,bl)+d(al,bh))
def small(a,b,dims=NT):
    return dot3(split(a),split(b),dims)
def factor_half(s_ref, a):
    rows=lax.broadcasted_iota(jnp.int32,(H,H),0); cols=lax.broadcasted_iota(jnp.int32,(H,H),1)
    s_ref[:, :H]=a
    s_ref[:, H:]=(rows==cols).astype(jnp.float32)
    sub=lax.broadcasted_iota(jnp.int32,(GRP,1),0)
    for g in range(H//GRP):
        j=g*GRP
        r=s_ref[j:j+GRP,:]
        cb=[jnp.broadcast_to(r[:,j+b:j+b+1],(GRP,H)) for b in range(GRP)]
        for i in range(GRP):
            rs=lax.rsqrt(cb[i][i:i+1,:])
            m=jnp.where(sub>i,cb[i]*rs,0.0)
            rs2=jnp.concatenate([rs,rs],axis=1); m2=jnp.concatenate([m,m],axis=1)
            u=r[i:i+1,:]*rs2
            r=jnp.where(sub==i,u,r-m2*u)
            for b in range(i+1,GRP):
                cb[b]=cb[b]-m*(cb[b][i:i+1,:]*rs)
        s_ref[j:j+GRP,:]=r
        if j+GRP<H:
            s_ref[j+GRP:,:]=s_ref[j+GRP:,:]-small(r[:,j+GRP:H],r,TN)
    u=jnp.where(rows<=cols,s_ref[:, :H],0.0)
    return u, s_ref[:, H:]

def factor_panel(nrow, ncol, g, ph, plo, inv, s_ref):
    def step(k, _):
        kc = pl.ds(pl.multiple_of(k * B, B), B)
        a = g[k, :, kc]
        u1, v1 = factor_half(s_ref, a[:H, :H])
        l21 = small(a[H:, :H], v1, NT)
        u2, v2 = factor_half(s_ref, a[H:, H:] - small(l21, l21, NT))
        zero = jnp.zeros((H, H), jnp.float32)
        inv[:H, :H] = v1
        inv[:H, H:] = zero
        inv[H:, :H] = -small(v2, small(l21, v1, NN), NN)
        inv[H:, H:] = v2
        g[k, :H, kc] = jnp.concatenate([u1.T, zero], axis=1)
        g[k, H:, kc] = jnp.concatenate([l21, u2.T], axis=1)
        iv = split(inv[...])

        def panel(i, _):
            p = dot3(split(g[i, :, kc]), iv)
            g[i, :, kc] = p
            ph[i], plo[i] = split(p)
            return 0

        lax.fori_loop(k + 1, nrow, panel, 0)

        def colup(j, _):
            jc = pl.ds(pl.multiple_of(j * B, B), B)
            w = (ph[j], plo[j])

            def rowup(i, _):
                g[i, :, jc] = g[i, :, jc] - dot3((ph[i], plo[i]), w)
                return 0

            lax.fori_loop(j, nrow, rowup, 0)
            return 0

        lax.fori_loop(k + 1, ncol, colup, 0)
        return 0

    lax.fori_loop(0, ncol, step, 0)


def panel_kernel(p, ntile, nown, sizes, *refs):
    tc, uc, ncol_dev = sizes
    per = PANEL // B
    first = p * per
    nrow = ntile - first + nown
    if p == 0:
        idx, d_ref, o_ref, out_ref, f_out, xh, xl, g, ph, plo, inv, s_ref = refs
    else:
        idx, d_ref, o_ref, d1_ref, o1_ref, f_in, out_ref, xh, xl, g, ph, plo, inv, s_ref = refs
    width = PANEL + uc * ncol_dev
    for i in range(nrow):
        t = i + first
        src = d_ref if t < ntile else o_ref
        at = (i if p else t) if t < ntile else t - ntile
        for c in range(ncol_dev):
            xh[i, :, c * tc : (c + 1) * tc], xl[i, :, c * tc : (c + 1) * tc] = split(src[at, c, :, :tc])
            lo = PANEL + c * uc
            xh[i, :, lo : lo + uc], xl[i, :, lo : lo + uc] = split(src[at, c, :, tc:])
        if p:
            src = d1_ref if t < ntile else o1_ref
            for c in range(ncol_dev):
                lo = width + c * tc
                xh[i, :, lo : lo + tc], xl[i, :, lo : lo + tc] = split(src[at, c])
            xh[i, :, width + PANEL :], xl[i, :, width + PANEL :] = split(f_in[i])
    full = width + p * PANEL

    def gram_col(j, _):
        jc = pl.ds(pl.multiple_of(j * B, B), B)

        def gram_row(i, _):
            v = dot3((xh[i, :, :full], xl[i, :, :full]), (xh[j, :, :full], xl[j, :, :full]))
            if p:
                v = v - dot3((xh[i, :, full:], xl[i, :, full:]), (xh[j, :, full:], xl[j, :, full:]))
            g[i, :, jc] = v
            return 0

        lax.fori_loop(j, nrow, gram_row, 0)
        return 0

    lax.fori_loop(0, per, gram_col, 0)
    factor_panel(nrow, per, g, ph, plo, inv, s_ref)
    if p == 0:
        f_out[...] = g[per:]
    oc = pl.ds(pl.multiple_of(idx[1] * tc, tc), tc)
    if nown == 1:
        r = idx[0] - first
        t = g[jnp.maximum(r, 0), :, oc]
        keep = idx[1] * (tc // B) <= r
        out_ref[0] = jnp.where(keep, t, 0.0)
        out_ref[1] = g[nrow - 1, :, oc]
    else:
        for e in range(2):
            out_ref[e] = g[nrow - 2 + e, :, oc]


def run_panel(p, idx, ntile, nown, sizes, *arrays):
    tc, uc, nc = sizes
    per = PANEL // B
    nrow = ntile - p * per + nown
    width = PANEL + uc * nc + p * 2 * PANEL
    vm = pl.BlockSpec(memory_space=pltpu.VMEM)
    shape = [jax.ShapeDtypeStruct((2, B, tc), jnp.float32)]
    if p == 0:
        shape.append(jax.ShapeDtypeStruct((nrow - per, B, PANEL), jnp.float32))
    return pl.pallas_call(
        functools.partial(panel_kernel, p, ntile, nown, sizes),
        out_shape=shape,
        in_specs=[pl.BlockSpec(memory_space=pltpu.SMEM)] + [vm] * len(arrays),
        out_specs=[vm] * len(shape),
        scratch_shapes=[
            pltpu.VMEM((nrow, B, width), jnp.bfloat16),
            pltpu.VMEM((nrow, B, width), jnp.bfloat16),
            pltpu.VMEM((nrow, B, PANEL), jnp.float32),
            pltpu.VMEM((nrow, B, B), jnp.bfloat16),
            pltpu.VMEM((nrow, B, B), jnp.bfloat16),
            pltpu.VMEM((B, B), jnp.float32),
            pltpu.VMEM((H, 2 * H), jnp.float32),
        ],
        cost_estimate=pl.CostEstimate(flops=60_000_000_000, bytes_accessed=30_000_000, transcendentals=0),
        compiler_params=pltpu.CompilerParams(vmem_limit_bytes=60 * 2**20),
        name="panel%d" % p,
    )(idx, *arrays)


def per_device(factor, update):
    blocks, tile_rows, panels, tc = factor.shape
    uc = update.shape[2]
    nr, nc = lax.axis_size("row"), lax.axis_size("col")
    r, c = lax.axis_index("row"), lax.axis_index("col")
    ntile = PANELS * PANEL // tile_rows
    whole_rows = nr == ntile
    nown = blocks - 1 if whole_rows else blocks
    sizes = (tc, uc, nc)
    xa = jnp.concatenate([factor[:, :, 0], update], axis=2)
    xb = factor[:, :, 1]

    def diag(x):
        if whole_rows:
            return lax.all_gather(x, ("row", "col")).reshape(ntile, nc, *x.shape)
        tiles = [lax.psum(jnp.where(r == t, x, 0.0), "row") for t in range(ntile)]
        return jnp.moveaxis(lax.all_gather(jnp.stack(tiles), "col"), 0, 1)

    def own(x):
        return jnp.moveaxis(lax.all_gather(x[blocks - nown :], "col"), 0, 1)

    da, oa = diag(xa[0]), own(xa)
    db, ob = diag(xb[0]), own(xb)
    idx = jnp.stack([r, c]).astype(jnp.int32)
    out0, f0 = run_panel(0, idx, ntile, nown, sizes, da, oa)
    (out1,) = run_panel(1, idx, ntile, nown, sizes, da[ntile // 2 :], oa, db[ntile // 2 :], ob, f0)
    out = jnp.stack([out0, out1], axis=2)
    if not whole_rows:
        rows = (
            jnp.arange(blocks)[:, None] * (nr * tile_rows) + r * tile_rows + jnp.arange(tile_rows)
        )
        cols = jnp.arange(panels)[:, None] * PANEL + c * tc + jnp.arange(tc)
        out = jnp.where(cols <= rows[:, :, None, None], out, 0.0)
    return out


def solution(mesh):
    in_specs = (P(None, "row", None, "col"), P(None, "row", "col"))
    out_specs = P(None, "row", None, "col")
    return jax.shard_map(
        per_device, mesh=mesh, in_specs=in_specs, out_specs=out_specs, check_vma=False
    )
```

```python
import functools

import jax
import jax.numpy as jnp
from jax import lax
from jax.experimental import pallas as pl
from jax.experimental.pallas import tpu as pltpu
from jax.sharding import PartitionSpec as P

PANEL = 1024
PANELS = 2
B=256; H=128; GRP=8
NN=(((1,),(0,)),((),()))
NT=(((1,),(1,)),((),())); TN=(((0,),(0,)),((),()))
def split(x):
    hi=x.astype(jnp.bfloat16); return hi,(x-hi.astype(jnp.float32)).astype(jnp.bfloat16)
def dot3(a,b,dims=NT):
    (ah,al),(bh,bl)=a,b
    d=functools.partial(lax.dot_general,dimension_numbers=dims,preferred_element_type=jnp.float32)
    return d(ah,bh)+(d(ah,bl)+d(al,bh))
def small(a,b,dims=NT):
    return dot3(split(a),split(b),dims)
def factor_half(s_ref, a):
    rows=lax.broadcasted_iota(jnp.int32,(H,H),0); cols=lax.broadcasted_iota(jnp.int32,(H,H),1)
    s_ref[:, :H]=a
    s_ref[:, H:]=(rows==cols).astype(jnp.float32)
    sub=lax.broadcasted_iota(jnp.int32,(GRP,1),0)
    for g in range(H//GRP):
        j=g*GRP
        r=s_ref[j:j+GRP,:]
        cb=[jnp.broadcast_to(r[:,j+b:j+b+1],(GRP,H)) for b in range(GRP)]
        for i in range(GRP):
            rs=lax.rsqrt(cb[i][i:i+1,:])
            m=jnp.where(sub>i,cb[i]*rs,0.0)
            rs2=jnp.concatenate([rs,rs],axis=1); m2=jnp.concatenate([m,m],axis=1)
            u=r[i:i+1,:]*rs2
            r=jnp.where(sub==i,u,r-m2*u)
            for b in range(i+1,GRP):
                cb[b]=cb[b]-m*(cb[b][i:i+1,:]*rs)
        s_ref[j:j+GRP,:]=r
        if j+GRP<H:
            s_ref[j+GRP:,:]=s_ref[j+GRP:,:]-small(r[:,j+GRP:H],r,TN)
    u=jnp.where(rows<=cols,s_ref[:, :H],0.0)
    return u, s_ref[:, H:]

def factor_panel(nrow, ncol, g, ph, plo, inv, s_ref):
    def step(k, _):
        kc = pl.ds(pl.multiple_of(k * B, B), B)
        a = g[k, :, kc]
        u1, v1 = factor_half(s_ref, a[:H, :H])
        l21 = small(a[H:, :H], v1, NT)
        u2, v2 = factor_half(s_ref, a[H:, H:] - small(l21, l21, NT))
        zero = jnp.zeros((H, H), jnp.float32)
        inv[:H, :H] = v1
        inv[:H, H:] = zero
        inv[H:, :H] = -small(v2, small(l21, v1, NN), NN)
        inv[H:, H:] = v2
        g[k, :H, kc] = jnp.concatenate([u1.T, zero], axis=1)
        g[k, H:, kc] = jnp.concatenate([l21, u2.T], axis=1)
        iv = split(inv[...])

        def panel(i, _):
            p = dot3(split(g[i, :, kc]), iv)
            g[i, :, kc] = p
            ph[i], plo[i] = split(p)
            return 0

        lax.fori_loop(k + 1, nrow, panel, 0)

        def colup(j, _):
            jc = pl.ds(pl.multiple_of(j * B, B), B)
            w = (ph[j], plo[j])

            def rowup(i, _):
                g[i, :, jc] = g[i, :, jc] - dot3((ph[i], plo[i]), w)
                return 0

            lax.fori_loop(j, nrow, rowup, 0)
            return 0

        lax.fori_loop(k + 1, ncol, colup, 0)
        return 0

    lax.fori_loop(0, ncol, step, 0)


def panel_kernel(p, ntile, nown, sizes, *refs):
    tc, uc, ncol_dev = sizes
    per = PANEL // B
    first = p * per
    nrow = ntile - first + nown
    if p == 0:
        idx, d_ref, o_ref, out_ref, f_out, xh, xl, g, ph, plo, inv, s_ref = refs
    else:
        idx, d_ref, o_ref, d1_ref, o1_ref, f_in, out_ref, xh, xl, g, ph, plo, inv, s_ref = refs
    width = PANEL + uc * ncol_dev
    for i in range(nrow):
        t = i + first
        src = d_ref if t < ntile else o_ref
        at = (i if p else t) if t < ntile else t - ntile
        for c in range(ncol_dev):
            xh[i, :, c * tc : (c + 1) * tc], xl[i, :, c * tc : (c + 1) * tc] = split(src[at, c, :, :tc])
            lo = PANEL + c * uc
            xh[i, :, lo : lo + uc], xl[i, :, lo : lo + uc] = split(src[at, c, :, tc:])
        if p:
            src = d1_ref if t < ntile else o1_ref
            for c in range(ncol_dev):
                lo = width + c * tc
                xh[i, :, lo : lo + tc], xl[i, :, lo : lo + tc] = split(src[at, c])
            xh[i, :, width + PANEL :], xl[i, :, width + PANEL :] = split(f_in[i])
    full = width + p * PANEL

    def gram_col(j, _):
        jc = pl.ds(pl.multiple_of(j * B, B), B)

        def gram_row(i, _):
            v = dot3((xh[i, :, :full], xl[i, :, :full]), (xh[j, :, :full], xl[j, :, :full]))
            if p:
                v = v - dot3((xh[i, :, full:], xl[i, :, full:]), (xh[j, :, full:], xl[j, :, full:]))
            g[i, :, jc] = v
            return 0

        lax.fori_loop(j, nrow, gram_row, 0)
        return 0

    lax.fori_loop(0, per, gram_col, 0)
    factor_panel(nrow, per, g, ph, plo, inv, s_ref)
    if p == 0:
        f_out[...] = g[per:]
    oc = pl.ds(pl.multiple_of(idx[1] * tc, tc), tc)
    if nown == 1:
        r = idx[0] - first
        t = g[jnp.maximum(r, 0), :, oc]
        keep = idx[1] * (tc // B) <= r
        out_ref[0] = jnp.where(keep, t, 0.0)
        out_ref[1] = g[nrow - 1, :, oc]
    else:
        for e in range(2):
            out_ref[e] = g[nrow - 2 + e, :, oc]


def run_panel(p, idx, ntile, nown, sizes, *arrays):
    tc, uc, nc = sizes
    per = PANEL // B
    nrow = ntile - p * per + nown
    width = PANEL + uc * nc + p * 2 * PANEL
    vm = pl.BlockSpec(memory_space=pltpu.VMEM)
    shape = [jax.ShapeDtypeStruct((2, B, tc), jnp.float32)]
    if p == 0:
        shape.append(jax.ShapeDtypeStruct((nrow - per, B, PANEL), jnp.float32))
    return pl.pallas_call(
        functools.partial(panel_kernel, p, ntile, nown, sizes),
        out_shape=shape,
        in_specs=[pl.BlockSpec(memory_space=pltpu.SMEM)] + [vm] * len(arrays),
        out_specs=[vm] * len(shape),
        scratch_shapes=[
            pltpu.VMEM((nrow, B, width), jnp.bfloat16),
            pltpu.VMEM((nrow, B, width), jnp.bfloat16),
            pltpu.VMEM((nrow, B, PANEL), jnp.float32),
            pltpu.VMEM((nrow, B, B), jnp.bfloat16),
            pltpu.VMEM((nrow, B, B), jnp.bfloat16),
            pltpu.VMEM((B, B), jnp.float32),
            pltpu.VMEM((H, 2 * H), jnp.float32),
        ],
        cost_estimate=pl.CostEstimate(flops=60_000_000_000, bytes_accessed=30_000_000, transcendentals=0),
        compiler_params=pltpu.CompilerParams(vmem_limit_bytes=60 * 2**20),
        name="panel%d" % p,
    )(idx, *arrays)


def per_device(factor, update):
    blocks, tile_rows, panels, tc = factor.shape
    uc = update.shape[2]
    nr, nc = lax.axis_size("row"), lax.axis_size("col")
    r, c = lax.axis_index("row"), lax.axis_index("col")
    ntile = PANELS * PANEL // tile_rows
    whole_rows = nr == ntile
    nown = blocks - 1 if whole_rows else blocks
    sizes = (tc, uc, nc)
    xa = jnp.concatenate([factor[:, :, 0], update], axis=2)
    xb = factor[:, :, 1]

    def diag(x):
        if whole_rows:
            return lax.all_gather(x, ("row", "col")).reshape(ntile, nc, *x.shape)
        tiles = [lax.psum(jnp.where(r == t, x, 0.0), "row") for t in range(ntile)]
        return jnp.moveaxis(lax.all_gather(jnp.stack(tiles), "col"), 0, 1)

    def own(x):
        return jnp.moveaxis(lax.all_gather(x[blocks - nown :], "col"), 0, 1)

    da, oa = diag(xa[0]), own(xa)
    xb = xb + (da[0, 0, 0, 0] + oa[0, 0, 0, 0]) * 0.0
    db, ob = diag(xb[0]), own(xb)
    idx = jnp.stack([r, c]).astype(jnp.int32)
    out0, f0 = run_panel(0, idx, ntile, nown, sizes, da, oa)
    (out1,) = run_panel(1, idx, ntile, nown, sizes, da[ntile // 2 :], oa, db[ntile // 2 :], ob, f0)
    out = jnp.stack([out0, out1], axis=2)
    if not whole_rows:
        rows = (
            jnp.arange(blocks)[:, None] * (nr * tile_rows) + r * tile_rows + jnp.arange(tile_rows)
        )
        cols = jnp.arange(panels)[:, None] * PANEL + c * tc + jnp.arange(tc)
        out = jnp.where(cols <= rows[:, :, None, None], out, 0.0)
    return out


def solution(mesh):
    in_specs = (P(None, "row", None, "col"), P(None, "row", "col"))
    out_specs = P(None, "row", None, "col")
    return jax.shard_map(
        per_device, mesh=mesh, in_specs=in_specs, out_specs=out_specs, check_vma=False
    )
```
